32 devices in a mesh: win: 2 (over x), row: 4 (over y, core), col: 4 (over z).
Axes of the slice: x: 2, y: 2, z: 4, core: 2. Of those that a mesh axis runs over, the one named last changes fastest.
Arguments:
- left_blocks: bfloat16 [16, 16, 16, 9216], P(('win', 'col'), 'row'), parts along dimension 0, may hold values from -0.15625 to 0.15625
- right_blocks: bfloat16 [16, 16, 16, 9216], P(('win', 'col'), 'row'), parts along dimension 0, may hold values from -12 to 12
- pattern: int32 [16, 16, 16], P(('win', 'col'), 'row'), parts along dimension 0, may hold values from 0 to 127, as said below
- left_live: int32 [16, 16, 16], P(('win', 'col'), 'row'), parts along dimension 0, may hold values from 0 to 1, as said below
- right_live: int32 [16, 16, 16], P(('win', 'col'), 'row'), parts along dimension 0, may hold values from 0 to 1, as said below
Outputs:
- next_iterate: bfloat16 [16, 16, 16, 9216], P(('win', 'col'), 'row'), parts along dimension 0
The draws below stay inside these ranges and needn't reach their ends.
There are 2 independent parts, one for each index of `win`. The reference program is written for one: setup_inputs(seed, part) draws one part's arguments, and reference() takes and returns one part's arrays. A program takes and returns all parts, laid end to end along the dimension named above; each array names one. Nothing has to cross between parts.
Inputs may be any that keep to these rules, and one draw needn't show every extreme that they name: Block row i = 16 x + y sits at cell (x, y) of a periodic 8 x 16 grid. pattern[x, y, 0] = i; the other 15 entries are distinct cells (x', y') other than (x, y), given as 16 x' + y', with x' - x and y' - y in -2 to 2 modulo 8 and 16. `left_live`: 1 marks a tile that the filter keeps. `right_live`: 1 marks a tile that the filter keeps.
All inputs are finite; a program needn't handle non-finite values.
Results may differ from the reference program's by a relative error of at most 0.001.
Values may be sent and summed in bfloat16 or wider, within the bound.
A program may use at most 128 MiB of HBM per device.

```python
import jax
import jax.numpy as jnp
from jax import lax

BS = 96
NG = 16
GX = 8
GY = 16


def draw_pattern(key, part):
    key = jax.random.fold_in(key, 11)
    window = jnp.arange(25, dtype=jnp.int32)
    others = jnp.concatenate([window[:12], window[13:]])
    step_x = others // 5 - 2
    step_y = others % 5 - 2
    scores = jax.random.randint(key, (GX, GY, 24), 0, 1 << 20) * 32 + jnp.arange(24, dtype=jnp.int32)
    order = jnp.argsort(scores, axis=2, stable=True)[:, :, :NG - 1]
    cell_x = jnp.arange(GX, dtype=jnp.int32)[:, None, None]
    cell_y = jnp.arange(GY, dtype=jnp.int32)[None, :, None]
    near_x = (cell_x + step_x[order]) % GX
    near_y = (cell_y + step_y[order]) % GY
    rest = near_x * GY + near_y
    own = jnp.broadcast_to(cell_x * GY + cell_y, (GX, GY, 1))
    return jnp.concatenate([own, rest], axis=2).astype(jnp.int32)


def draw_left_live(key, part):
    key = jax.random.fold_in(key, 23)
    scores = jax.random.randint(key, (GX, GY, NG), 0, 100)
    limits = 20 + 70 * jnp.arange(GX) // GX
    return (scores < limits[:, None, None]).astype(jnp.int32)


def draw_right_live(key, part):
    key = jax.random.fold_in(key, 37)
    scores = jax.random.randint(key, (GX, GY, NG), 0, 100)
    limits = 90 - 60 * jnp.arange(GX) // GX
    return (scores < limits[:, None, None]).astype(jnp.int32)


def level_of(rng, shape, cuts, smallest, top_value):
    def one(axis_at, blocks):
        draws = jax.random.uniform(jax.random.fold_in(jax.random.fold_in(rng, 6), axis_at), (blocks,), jnp.float32, smallest / len(cuts), top_value / len(cuts))
        return jnp.repeat(jnp.exp(draws), shape[axis_at] // blocks).reshape((-1,) + (1,) * (len(shape) - axis_at - 1))

    gain = one(*cuts[0])
    for cut in cuts[1:]:
        gain = gain * one(*cut)
    return gain


def centred(stream_key, extent, scale, limit, cuts=(), held_as=jnp.bfloat16):
    drawn = scale * jax.random.normal(stream_key, extent, jnp.float32)
    if cuts:
        drawn = drawn * level_of(stream_key, extent, cuts, -0.22, 0.18)
    return jnp.clip(drawn, -limit, limit).astype(held_as)


def setup_inputs(seed: int = 0, part: int = 0) -> dict:
    key_list = jax.random.split(jax.random.key(seed), 6)
    own_keys = jax.random.split(jax.random.fold_in(key_list[5], part), 6)
    return {
        "left_blocks": centred(own_keys[0], (GX, GY, NG, BS * BS), (NG * BS) ** -0.5, 0.15625, ((0, 4), (1, 4))),
        "right_blocks": centred(own_keys[1], (GX, GY, NG, BS * BS), 2.0, 12.0, ((0, 4), (1, 4))),
        "pattern": draw_pattern(jax.random.fold_in(jax.random.fold_in(key_list[5], part), 71), part),
        "left_live": draw_left_live(jax.random.fold_in(jax.random.fold_in(key_list[5], part), 71), part),
        "right_live": draw_right_live(jax.random.fold_in(jax.random.fold_in(key_list[5], part), 71), part),
    }


def reference(left_blocks, right_blocks, pattern, left_live, right_live):
    grid_x, grid_y, slot_count, tile_area = left_blocks.shape
    total_blocks = grid_x * grid_y
    left_view = left_blocks.reshape(total_blocks, slot_count, BS, BS)
    right_view = right_blocks.reshape(total_blocks, slot_count, BS, BS)
    flat_pattern = pattern.reshape(total_blocks, slot_count).astype(jnp.int32)
    left_mask = left_live.reshape(total_blocks, slot_count).astype(jnp.float32)
    right_mask = right_live.reshape(total_blocks, slot_count).astype(jnp.float32)
    slot_ids = jnp.arange(slot_count, dtype=jnp.int32)

    def one_slot(target_slot):
        wanted = flat_pattern[:, target_slot]

        def add_group(running, group_index):
            neighbour = flat_pattern[:, group_index]
            neighbour_cols = flat_pattern[neighbour]
            match = neighbour_cols == wanted[:, None]
            chosen = jnp.sum(jnp.where(match, slot_ids[None, :], 0), axis=1).astype(jnp.int32)
            present = jnp.any(match, axis=1)
            tiles = right_view[neighbour, chosen].astype(jnp.float32)
            weight = jnp.where(present, right_mask[neighbour, chosen], jnp.float32(0.0))
            tiles = tiles * weight[:, None, None]
            left_tiles = left_view[:, group_index].astype(jnp.float32) * left_mask[:, group_index][:, None, None]
            return running + jnp.einsum("nab,nbc->nac", left_tiles, tiles), None

        start_sum = jnp.zeros((total_blocks, BS, BS), jnp.float32)
        total, unused_out = lax.scan(add_group, start_sum, slot_ids)
        return (0.5 * total).astype(jnp.bfloat16)

    results = lax.map(one_slot, slot_ids)
    results = jnp.moveaxis(results, 0, 1)
    return results.reshape(grid_x, grid_y, slot_count, tile_area)
```

```python
import functools

import jax
import jax.numpy as jnp
from jax import lax
from jax.experimental import pallas as pl
from jax.experimental.pallas import tpu as pltpu
from jax.sharding import PartitionSpec as P

BS = 96
LANES = 128
REACH = 2
GROUP = 2


def shift(array, axis, step):
    peers = lax.axis_size(axis)
    return lax.ppermute(array, axis, [(i, (i + step) % peers) for i in range(peers)])


def halo(low, high):
    own = (low, high)
    before_x = [shift(p, "col", 1) for p in own]
    after_x = [shift(p, "col", -1) for p in own]
    rows = []
    for mid in (before_x, own, after_x):
        rows.append([shift(mid[1], "row", 1), mid[0], mid[1], shift(mid[0], "row", -1)])
    return rows


def product_kernel(slots, pieces, *refs):
    table = refs[0]
    left = refs[1]
    sources = refs[2 : 2 + pieces]
    out = refs[2 + pieces]
    near, wide_a, wide_b, sems = refs[3 + pieces :]
    span = near.shape[0] // pieces
    copies = [
        pltpu.make_async_copy(src, near.at[pl.ds(n * span, span)], sems.at[n])
        for n, src in enumerate(sources)
    ]
    for copy in copies:
        copy.start()
    for copy in copies:
        copy.wait()
    buffers = (wide_a, wide_b)
    rows = left.shape[0]

    def gather(row, first, wide):
        for g in range(slots):
            for u in range(GROUP):
                at = table[(row * slots + g) * slots + first + u]
                tile = near[jnp.maximum(at, 0)]
                tile = jnp.where(at >= 0, tile, jnp.zeros_like(tile))
                wide[g * BS : (g + 1) * BS, u * LANES : u * LANES + BS] = tile

    def one_row(row, carry):
        lhs = left[row]
        turns = slots // GROUP
        for turn in range(turns):
            wide = buffers[turn % 2]
            gather(row, turn * GROUP, wide)
            total = jnp.dot(lhs, wide[...], preferred_element_type=jnp.float32)
            total = (0.5 * total).astype(out.dtype)
            for u in range(GROUP):
                out[row, turn * GROUP + u] = total[:, u * LANES : u * LANES + BS]
        return carry

    lax.fori_loop(0, rows, one_row, 0)


def body(left_blocks, right_blocks, pattern, left_live, right_live):
    cells_x, cells_y, slots, area = left_blocks.shape
    rows = cells_x * cells_y
    assert cells_x == REACH and cells_y == 2 * REACH
    grid_x = cells_x * lax.axis_size("col")
    grid_y = cells_y * lax.axis_size("row")

    codes = pattern * 2 + (right_live != 0).astype(jnp.int32)
    code_pieces = halo(codes[:, :REACH], codes[:, REACH:])
    tile_pieces = halo(right_blocks[:, :REACH], right_blocks[:, REACH:])
    cells = REACH * REACH
    near_codes = jnp.concatenate(
        [p.reshape(cells, slots) for line in code_pieces for p in line], axis=0
    )
    sources = [
        p.reshape(cells * slots, BS, BS) for line in tile_pieces for p in line
    ]

    local_x = jnp.arange(cells_x, dtype=jnp.int32)[:, None, None]
    local_y = jnp.arange(cells_y, dtype=jnp.int32)[None, :, None]
    own_x = lax.axis_index("col") * cells_x + local_x
    own_y = lax.axis_index("row") * cells_y + local_y
    near_x = local_x + (pattern // grid_y - own_x + REACH) % grid_x
    near_y = local_y + (pattern % grid_y - own_y + REACH) % grid_y
    piece = (near_x // REACH) * 4 + near_y // REACH
    place = piece * cells + (near_x % REACH) * REACH + near_y % REACH
    place = place.reshape(rows, slots)
    targets = pattern.reshape(rows, slots)
    picked = near_codes[place]
    live = (picked % 2 == 1) & (left_live.reshape(rows, slots) != 0)[:, :, None]
    match = (picked[:, :, None, :] // 2 == targets[:, None, :, None]) & live[:, :, None, :]
    found = jnp.where(match, jnp.arange(slots, dtype=jnp.int32) + 1, 0).max(axis=3)
    table = jnp.where(found > 0, place[:, :, None] * slots + found - 1, -1).reshape(-1)

    left = left_blocks.reshape(rows, slots, BS, BS)
    left = jnp.moveaxis(left, 1, 2).reshape(rows, BS, slots * BS)

    count = len(sources)
    vmem = pl.BlockSpec(memory_space=pltpu.VMEM)
    out = pl.pallas_call(
        functools.partial(product_kernel, slots, count),
        out_shape=jax.ShapeDtypeStruct((rows, slots, BS, BS), jnp.bfloat16),
        in_specs=[pl.BlockSpec(memory_space=pltpu.SMEM), vmem]
        + [pl.BlockSpec(memory_space=pl.ANY)] * count,
        out_specs=vmem,
        scratch_shapes=[
            pltpu.VMEM((count * cells * slots, BS, BS), jnp.bfloat16),
            pltpu.VMEM((slots * BS, GROUP * LANES), jnp.bfloat16),
            pltpu.VMEM((slots * BS, GROUP * LANES), jnp.bfloat16),
            pltpu.SemaphoreType.DMA((count,)),
        ],
        compiler_params=pltpu.CompilerParams(vmem_limit_bytes=36 * 1024 * 1024),
        cost_estimate=pl.CostEstimate(
            flops=2 * rows * slots * slots * BS**3,
            bytes_accessed=2 * (count * cells + 2 * rows) * slots * area,
            transcendentals=0,
        ),
    )(table, left, *sources)
    return out.reshape(cells_x, cells_y, slots, area)


def solution(mesh):
    placed = (
        P(("win", "col"), "row", None, None),
        P(("win", "col"), "row", None, None),
        P(("win", "col"), "row", None),
        P(("win", "col"), "row", None),
        P(("win", "col"), "row", None),
    )
    return jax.shard_map(
        body,
        mesh=mesh,
        in_specs=placed,
        out_specs=P(("win", "col"), "row", None, None),
        check_vma=False,
    )
```

```python
import functools

import jax
import jax.numpy as jnp
from jax import lax
from jax.experimental import pallas as pl
from jax.experimental.pallas import tpu as pltpu
from jax.sharding import PartitionSpec as P

BS = 96
LANES = 128
REACH = 2
GROUP = 2


HALF = BS // 2
PAIR_ROWS = 3 * HALF
WIDE = 64
CHUNKS = 2
MESH = pl.DeviceIdType.MESH


def pack(first, second):
    parts = [first[:HALF, :WIDE], first[HALF:, :WIDE]]
    others = [second[:HALF, :WIDE], second[HALF:, :WIDE]]
    narrow = [t[h : h + HALF, WIDE:] for t in (first, second) for h in (0, HALF)]
    return [jnp.concatenate(p, axis=1) for p in (parts, others, narrow)]


def unpack(rows_0, rows_1, narrow):
    step = BS - WIDE
    return [
        jnp.concatenate(
            [rows[:, h * WIDE : (h + 1) * WIDE], narrow[:, n * step : (n + 1) * step]], axis=1
        )
        for n, (rows, h) in enumerate(((rows_0, 0), (rows_0, 1), (rows_1, 0), (rows_1, 1)))
    ]


def halo_kernel(cells_y, slots, peers_col, peers_row, tiles, codes, near, near_codes, own, *sems):
    send_sems, recv_sems, code_send, code_recv, local_sems = sems
    col = lax.axis_index("col")
    row = lax.axis_index("row")
    up = {"col": lax.rem(col + 1, peers_col)}
    down = {"col": lax.rem(col + peers_col - 1, peers_col)}
    right = {"row": lax.rem(row + 1, peers_row)}
    back = {"row": lax.rem(row + peers_row - 1, peers_row)}

    barrier = pltpu.get_barrier_semaphore()
    for peer in (up, down, right, back):
        pl.semaphore_signal(barrier, inc=1, device_id=peer, device_id_type=MESH)

    pairs = slots // 2

    def pack_half(half):
        for x in range(REACH):
            for y in range(REACH):
                source = (x * cells_y + half * REACH + y) * slots
                target = (x * REACH + y) * pairs

                def one(p, carry):
                    blocks = pack(tiles[source + 2 * p], tiles[source + 2 * p + 1])
                    for n, block in enumerate(blocks):
                        own[half, target + p, n * HALF : (n + 1) * HALF, :] = block
                    return carry

                lax.fori_loop(0, pairs, one, 0)

    pack_half(0)
    pack_half(1)
    pl.semaphore_wait(barrier, 4)

    first_hop = [(0, 1, 0, up), (2, 1, 0, down), (0, 2, 1, up), (2, 2, 1, down)]
    side_hop = [(1, 3, 0, back), (1, 0, 1, right)]
    span = own.shape[1] // CHUNKS

    def move(place, chunk, source, device, count):
        part = pl.ds(chunk * span, span)
        return pltpu.make_async_remote_copy(
            src_ref=source.at[part],
            dst_ref=near.at[place, part],
            send_sem=send_sems.at[count],
            recv_sem=recv_sems.at[place, chunk],
            device_id=device,
            device_id_type=MESH,
        )

    def move_code(place, source, device, count):
        return pltpu.make_async_remote_copy(
            src_ref=source,
            dst_ref=near_codes.at[place],
            send_sem=code_send.at[count],
            recv_sem=code_recv.at[place],
            device_id=device,
            device_id_type=MESH,
        )

    code_moves = []
    for px, py, half, device in first_hop + side_hop:
        code_moves.append(move_code(px * 4 + py, codes.at[half], device, len(code_moves)))
    for m in code_moves:
        m.start()

    moves = []
    chain = []
    for px, py, half, device in first_hop:
        for chunk in range(CHUNKS):
            m = move(px * 4 + py, chunk, own.at[half], device, len(moves))
            moves.append(m)
            chain.append((m, px, py, chunk))
    order = []
    for n in range(0, len(first_hop), 2):
        for chunk in range(CHUNKS):
            order.append(chain[n * CHUNKS + chunk])
            order.append(chain[(n + 1) * CHUNKS + chunk])
    sides = []
    for chunk in range(CHUNKS):
        for px, py, half, device in side_hop:
            m = move(px * 4 + py, chunk, own.at[half], device, len(moves))
            moves.append(m)
            sides.append(m)
    ahead = 4
    for m, *_ in order[:ahead]:
        m.start()
    for m in sides:
        m.start()
    locals_ = []
    for half in range(2):
        locals_.append(
            pltpu.make_async_copy(own.at[half], near.at[4 + 1 + half], local_sems.at[half])
        )
        locals_.append(
            pltpu.make_async_copy(codes.at[half], near_codes.at[4 + 1 + half], local_sems.at[2 + half])
        )
    for m in locals_:
        m.start()

    code_forwards = []
    for n, (px, py, half, device) in enumerate(first_hop):
        code_moves[n].wait_recv()
        target, device = ((px * 4 + 3), back) if py == 1 else (px * 4, right)
        m = move_code(target, near_codes.at[px * 4 + py], device, len(code_moves) + n)
        m.start()
        code_forwards.append(m)

    forwards = []
    for n, (m, px, py, chunk) in enumerate(order):
        m.wait_recv()
        target, device = ((px * 4 + 3), back) if py == 1 else (px * 4, right)
        f = move(target, chunk, near.at[px * 4 + py], device, len(moves) + n)
        f.start()
        forwards.append(f)
        if n + ahead < len(order):
            order[n + ahead][0].start()
    for m in sides + forwards + code_moves[4:] + code_forwards:
        m.wait_recv()
    for m in moves + forwards + code_moves + code_forwards:
        m.wait_send()
    for m in locals_:
        m.wait()


def product_kernel(slots, table, left, packed, out, near, raw, wide_a, wide_b, sems):
    pieces, pairs = packed.shape[:2]

    def fetch(n):
        return pltpu.make_async_copy(packed.at[n], raw.at[n % 2], sems.at[n % 2])

    fetch(0).start()
    for n in range(pieces):
        if n + 1 < pieces:
            fetch(n + 1).start()
        fetch(n).wait()

        def one_pair(p, carry):
            blocks = [raw[n % 2, p, k * HALF : (k + 1) * HALF, :] for k in range(3)]
            halves = unpack(*blocks)
            at = (n * pairs + p) * 2
            for k, half in enumerate(halves):
                near[at + k // 2, (k % 2) * HALF : (k % 2 + 1) * HALF, :] = half
            return carry

        lax.fori_loop(0, pairs, one_pair, 0, unroll=2)

    buffers = (wide_a, wide_b)
    rows = left.shape[0]

    def gather(row, first, wide):
        for g in range(slots):
            for u in range(GROUP):
                at = table[(row * slots + g) * slots + first + u]
                tile = near[jnp.maximum(at, 0)]
                tile = jnp.where(at >= 0, tile, jnp.zeros_like(tile))
                wide[g * BS : (g + 1) * BS, u * LANES : u * LANES + BS] = tile

    def one_row(row, carry):
        lhs = left[row]
        turns = slots // GROUP
        for turn in range(turns):
            wide = buffers[turn % 2]
            gather(row, turn * GROUP, wide)
            total = jnp.dot(lhs, wide[...], preferred_element_type=jnp.float32)
            total = (0.5 * total).astype(out.dtype)
            for u in range(GROUP):
                out[row, turn * GROUP + u] = total[:, u * LANES : u * LANES + BS]
        return carry

    lax.fori_loop(0, rows, one_row, 0)


def body(left_blocks, right_blocks, pattern, left_live, right_live):
    cells_x, cells_y, slots, area = left_blocks.shape
    rows = cells_x * cells_y
    assert cells_x == REACH and cells_y == 2 * REACH
    peers_col = lax.axis_size("col")
    peers_row = lax.axis_size("row")
    grid_x = cells_x * peers_col
    grid_y = cells_y * peers_row
    cells = REACH * REACH
    pieces = 12
    pairs = cells * slots // 2
    vmem = pl.BlockSpec(memory_space=pltpu.VMEM)
    anywhere = pl.BlockSpec(memory_space=pl.ANY)

    codes = pattern * 2 + (right_live != 0).astype(jnp.int32)
    codes = jnp.stack([codes[:, :REACH], codes[:, REACH:]]).reshape(2, cells, slots)
    codes = jnp.pad(codes, ((0, 0), (0, 8 - cells), (0, LANES - slots)))
    count = 6 * CHUNKS + 4 * CHUNKS
    packed, near_codes = pl.pallas_call(
        functools.partial(halo_kernel, cells_y, slots, peers_col, peers_row),
        out_shape=(
            jax.ShapeDtypeStruct((pieces, pairs, PAIR_ROWS, LANES), jnp.bfloat16),
            jax.ShapeDtypeStruct((pieces, 8, LANES), jnp.int32),
        ),
        in_specs=[vmem, vmem],
        out_specs=(anywhere, anywhere),
        scratch_shapes=[
            pltpu.VMEM((2, pairs, PAIR_ROWS, LANES), jnp.bfloat16),
            pltpu.SemaphoreType.DMA((count,)),
            pltpu.SemaphoreType.DMA((pieces, CHUNKS)),
            pltpu.SemaphoreType.DMA((10,)),
            pltpu.SemaphoreType.DMA((pieces,)),
            pltpu.SemaphoreType.DMA((4,)),
        ],
        compiler_params=pltpu.CompilerParams(
            collective_id=0, has_side_effects=True, vmem_limit_bytes=16 * 1024 * 1024
        ),
        cost_estimate=pl.CostEstimate(
            flops=0, bytes_accessed=2 * pieces * cells * slots * area, transcendentals=0
        ),
    )(right_blocks.reshape(rows * slots, BS, BS), codes)
    near_codes = near_codes[:, :cells, :slots].reshape(pieces * cells, slots)

    local_x = jnp.arange(cells_x, dtype=jnp.int32)[:, None, None]
    local_y = jnp.arange(cells_y, dtype=jnp.int32)[None, :, None]
    own_x = lax.axis_index("col") * cells_x + local_x
    own_y = lax.axis_index("row") * cells_y + local_y
    near_x = local_x + (pattern // grid_y - own_x + REACH) % grid_x
    near_y = local_y + (pattern % grid_y - own_y + REACH) % grid_y
    piece = (near_x // REACH) * 4 + near_y // REACH
    place = piece * cells + (near_x % REACH) * REACH + near_y % REACH
    place = place.reshape(rows, slots)
    targets = pattern.reshape(rows, slots)
    picked = near_codes[place]
    live = (picked % 2 == 1) & (left_live.reshape(rows, slots) != 0)[:, :, None]
    match = (picked[:, :, None, :] // 2 == targets[:, None, :, None]) & live[:, :, None, :]
    found = jnp.where(match, jnp.arange(slots, dtype=jnp.int32) + 1, 0).max(axis=3)
    table = jnp.where(found > 0, place[:, :, None] * slots + found - 1, -1).reshape(-1)

    left = left_blocks.reshape(rows, slots, BS, BS)
    left = jnp.moveaxis(left, 1, 2).reshape(rows, BS, slots * BS)

    out = pl.pallas_call(
        functools.partial(product_kernel, slots),
        out_shape=jax.ShapeDtypeStruct((rows, slots, BS, BS), jnp.bfloat16),
        in_specs=[pl.BlockSpec(memory_space=pltpu.SMEM), vmem, anywhere],
        out_specs=vmem,
        scratch_shapes=[
            pltpu.VMEM((pieces * cells * slots, BS, BS), jnp.bfloat16),
            pltpu.VMEM((2, pairs, PAIR_ROWS, LANES), jnp.bfloat16),
            pltpu.VMEM((slots * BS, GROUP * LANES), jnp.bfloat16),
            pltpu.VMEM((slots * BS, GROUP * LANES), jnp.bfloat16),
            pltpu.SemaphoreType.DMA((2,)),
        ],
        compiler_params=pltpu.CompilerParams(vmem_limit_bytes=36 * 1024 * 1024),
        cost_estimate=pl.CostEstimate(
            flops=2 * rows * slots * slots * BS**3,
            bytes_accessed=2 * (pieces * cells + 2 * rows) * slots * area,
            transcendentals=0,
        ),
    )(table, left, packed)
    return out.reshape(cells_x, cells_y, slots, area)


def solution(mesh):
    placed = (
        P(("win", "col"), "row", None, None),
        P(("win", "col"), "row", None, None),
        P(("win", "col"), "row", None),
        P(("win", "col"), "row", None),
        P(("win", "col"), "row", None),
    )
    return jax.shard_map(
        body,
        mesh=mesh,
        in_specs=placed,
        out_specs=P(("win", "col"), "row", None, None),
        check_vma=False,
    )
```

```python
import functools

import jax
import jax.numpy as jnp
from jax import lax
from jax.experimental import pallas as pl
from jax.experimental.pallas import tpu as pltpu
from jax.sharding import PartitionSpec as P

BS = 96
LANES = 128
REACH = 2
GROUP = 2


HALF = BS // 2
PAIR_ROWS = 3 * HALF
WIDE = 64
CHUNKS = 2
MESH = pl.DeviceIdType.MESH


def pack(first, second):
    parts = [first[:HALF, :WIDE], first[HALF:, :WIDE]]
    others = [second[:HALF, :WIDE], second[HALF:, :WIDE]]
    narrow = [t[h : h + HALF, WIDE:] for t in (first, second) for h in (0, HALF)]
    return [jnp.concatenate(p, axis=1) for p in (parts, others, narrow)]


def unpack(rows_0, rows_1, narrow):
    step = BS - WIDE
    return [
        jnp.concatenate(
            [rows[:, h * WIDE : (h + 1) * WIDE], narrow[:, n * step : (n + 1) * step]], axis=1
        )
        for n, (rows, h) in enumerate(((rows_0, 0), (rows_0, 1), (rows_1, 0), (rows_1, 1)))
    ]


def near_kernel(
    cells_y, slots, peers_col, peers_row,
    place, tiles, left, codes, targets,
    out,
    packed, near, near_codes, table_rows, table, stacked, wide_a, wide_b, *sems,
):
    send_sems, recv_sems, code_send, code_recv, table_sem = sems
    col = lax.axis_index("col")
    row = lax.axis_index("row")
    up = {"col": lax.rem(col + 1, peers_col)}
    down = {"col": lax.rem(col + peers_col - 1, peers_col)}
    right = {"row": lax.rem(row + 1, peers_row)}
    back = {"row": lax.rem(row + peers_row - 1, peers_row)}
    pairs = slots // 2
    piece_pairs = packed.shape[1]
    span = piece_pairs // CHUNKS
    cells = REACH * REACH
    rows = out.shape[0]

    barrier = pltpu.get_barrier_semaphore()
    for peer in (up, down, right, back):
        pl.semaphore_signal(barrier, inc=1, device_id=peer, device_id_type=MESH)

    def pack_half(half):
        for x in range(REACH):
            for y in range(REACH):
                source = (x * cells_y + half * REACH + y) * slots
                target = (x * REACH + y) * pairs

                def one(p, carry):
                    first, second = tiles[source + 2 * p], tiles[source + 2 * p + 1]
                    for n, block in enumerate(pack(first, second)):
                        packed[5 + half, target + p, n * HALF : (n + 1) * HALF, :] = block
                    at = ((5 + half) * piece_pairs + target + p) * 2
                    near[at] = first
                    near[at + 1] = second
                    return carry

                lax.fori_loop(0, pairs, one, 0)

    def unpack_chunk(at_piece, chunk):
        def one(p, carry):
            blocks = [
                packed[at_piece, chunk * span + p, k * HALF : (k + 1) * HALF, :] for k in range(3)
            ]
            at = (at_piece * piece_pairs + chunk * span + p) * 2
            for k, half in enumerate(unpack(*blocks)):
                near[at + k // 2, (k % 2) * HALF : (k % 2 + 1) * HALF, :] = half
            return carry

        lax.fori_loop(0, span, one, 0)

    def move(to, chunk, source, device, count):
        part = pl.ds(chunk * span, span)
        return pltpu.make_async_remote_copy(
            src_ref=packed.at[source, part],
            dst_ref=packed.at[to, part],
            send_sem=send_sems.at[count],
            recv_sem=recv_sems.at[to, chunk],
            device_id=device,
            device_id_type=MESH,
        )

    def move_code(to, source, device, count):
        return pltpu.make_async_remote_copy(
            src_ref=source,
            dst_ref=near_codes.at[pl.ds(to * cells, cells)],
            send_sem=code_send.at[count],
            recv_sem=code_recv.at[to],
            device_id=device,
            device_id_type=MESH,
        )

    first_hop = [(0, 1, 0, up), (2, 1, 0, down), (0, 2, 1, up), (2, 2, 1, down)]
    side_hop = [(1, 3, 0, back), (1, 0, 1, right)]
    code_moves = []
    for px, py, half, device in first_hop + side_hop:
        code_moves.append(move_code(px * 4 + py, codes.at[half], device, len(code_moves)))
    moves = []
    order = []
    for n in range(0, len(first_hop), 2):
        for chunk in range(CHUNKS):
            for px, py, half, device in first_hop[n : n + 2]:
                m = move(px * 4 + py, chunk, 5 + half, device, len(moves))
                moves.append(m)
                order.append((m, px, py, chunk))
    sides = []
    for px, py, half, device in side_hop:
        for chunk in range(CHUNKS):
            m = move(px * 4 + py, chunk, 5 + half, device, len(moves))
            moves.append(m)
            sides.append((m, px * 4 + py, chunk))

    pack_half(0)
    pl.semaphore_wait(barrier, 4)
    ahead = 2 * CHUNKS
    for m in code_moves:
        m.start()
    for m, *_ in order[:ahead]:
        m.start()
    for m, *_ in sides[:CHUNKS]:
        m.start()
    pack_half(1)
    for m, *_ in sides[CHUNKS:]:
        m.start()

    def stack_row(i, carry):
        for g in range(0, slots, 4):
            parts = [left[i * slots + g + u] for u in range(4)]
            stacked[i, :, g * BS : (g + 4) * BS] = jnp.concatenate(parts, axis=1)
        return carry

    near_codes[5 * cells : 7 * cells] = codes[...].reshape(2 * cells, *codes.shape[2:])
    code_forwards = []
    for n, (px, py, half, device) in enumerate(first_hop):
        code_moves[n].wait_recv()
        to, device = ((px * 4 + 3), back) if py == 1 else (px * 4, right)
        source = near_codes.at[pl.ds((px * 4 + py) * cells, cells)]
        m = move_code(to, source, device, len(code_moves) + n)
        m.start()
        code_forwards.append(m)
    lax.fori_loop(0, rows, stack_row, 0)
    for m in code_moves[4:] + code_forwards:
        m.wait_recv()

    slot_rows = lax.broadcasted_iota(jnp.int32, (slots, LANES), 0)

    def table_row(n, carry):
        at = place[n]
        held = near_codes[jnp.maximum(at, 0)]
        match = (lax.shift_right_logical(held, 1) == targets[n // slots]) & ((held & 1) == 1)
        found = jnp.max(jnp.where(match, slot_rows + 1, 0), axis=0, keepdims=True)
        good = (found > 0) & (at >= 0)
        table_rows[pl.ds(n, 1)] = jnp.where(good, at * slots + found - 1, -1)
        return carry

    lax.fori_loop(0, rows * slots, table_row, 0)
    table_copy = pltpu.make_async_copy(table_rows, table, table_sem)
    table_copy.start()

    forwards = []
    for n, (m, px, py, chunk) in enumerate(order):
        m.wait_recv()
        to, device = ((px * 4 + 3), back) if py == 1 else (px * 4, right)
        f = move(to, chunk, px * 4 + py, device, len(moves) + n)
        f.start()
        forwards.append((f, to, chunk))
        if n + ahead < len(order):
            order[n + ahead][0].start()
        unpack_chunk(px * 4 + py, chunk)
        if n < len(sides):
            sides[n][0].wait_recv()
            unpack_chunk(*sides[n][1:])
        if n >= 2:
            forwards[n - 2][0].wait_recv()
            unpack_chunk(*forwards[n - 2][1:])
    for f, to, chunk in forwards[-2:]:
        f.wait_recv()
        unpack_chunk(to, chunk)
    table_copy.wait()

    buffers = (wide_a, wide_b)

    def gather(i, first, wide):
        for g in range(slots):
            for u in range(GROUP):
                at = table[i * slots + g, first + u]
                tile = near[jnp.maximum(at, 0)]
                tile = jnp.where(at >= 0, tile, jnp.zeros_like(tile))
                wide[g * BS : (g + 1) * BS, u * LANES : u * LANES + BS] = tile

    def one_row(i, carry):
        lhs = stacked[i]
        for turn in range(slots // GROUP):
            wide = buffers[turn % 2]
            gather(i, turn * GROUP, wide)
            total = jnp.dot(lhs, wide[...], preferred_element_type=jnp.float32)
            total = (0.5 * total).astype(out.dtype)
            for u in range(GROUP):
                out[i, turn * GROUP + u] = total[:, u * LANES : u * LANES + BS]
        return carry

    wide_a[...] = jnp.zeros_like(wide_a)
    wide_b[...] = jnp.zeros_like(wide_b)
    lax.fori_loop(0, rows, one_row, 0)
    for m in moves + [f for f, *_ in forwards] + code_moves + code_forwards:
        m.wait_send()


def body(left_blocks, right_blocks, pattern, left_live, right_live):
    cells_x, cells_y, slots, area = left_blocks.shape
    rows = cells_x * cells_y
    assert cells_x == REACH and cells_y == 2 * REACH
    peers_col = lax.axis_size("col")
    peers_row = lax.axis_size("row")
    grid_x = cells_x * peers_col
    grid_y = cells_y * peers_row
    cells = REACH * REACH
    pieces = 12
    piece_pairs = cells * slots // 2
    vmem = pl.BlockSpec(memory_space=pltpu.VMEM)

    codes = pattern * 2 + (right_live != 0).astype(jnp.int32)
    codes = jnp.stack([codes[:, :REACH], codes[:, REACH:]]).reshape(2, cells, slots, 1)
    codes = jnp.broadcast_to(codes, (2, cells, slots, LANES))

    local_x = jnp.arange(cells_x, dtype=jnp.int32)[:, None, None]
    local_y = jnp.arange(cells_y, dtype=jnp.int32)[None, :, None]
    own_x = lax.axis_index("col") * cells_x + local_x
    own_y = lax.axis_index("row") * cells_y + local_y
    near_x = local_x + (pattern // grid_y - own_x + REACH) % grid_x
    near_y = local_y + (pattern % grid_y - own_y + REACH) % grid_y
    piece = (near_x // REACH) * 4 + near_y // REACH
    place = piece * cells + (near_x % REACH) * REACH + near_y % REACH
    place = jnp.where(left_live != 0, place, -1).reshape(-1)
    targets = jnp.pad(
        pattern.reshape(rows, 1, slots), ((0, 0), (0, 0), (0, LANES - slots)), constant_values=-1
    )

    count = 10 * CHUNKS
    out = pl.pallas_call(
        functools.partial(near_kernel, cells_y, slots, peers_col, peers_row),
        out_shape=jax.ShapeDtypeStruct((rows, slots, BS, BS), jnp.bfloat16),
        in_specs=[pl.BlockSpec(memory_space=pltpu.SMEM), vmem, vmem, vmem, vmem],
        out_specs=vmem,
        scratch_shapes=[
            pltpu.VMEM((pieces, piece_pairs, PAIR_ROWS, LANES), jnp.bfloat16),
            pltpu.VMEM((pieces * cells * slots, BS, BS), jnp.bfloat16),
            pltpu.VMEM((pieces * cells, slots, LANES), jnp.int32),
            pltpu.VMEM((rows * slots, LANES), jnp.int32),
            pltpu.SMEM((rows * slots, LANES), jnp.int32),
            pltpu.VMEM((rows, BS, slots * BS), jnp.bfloat16),
            pltpu.VMEM((slots * BS, GROUP * LANES), jnp.bfloat16),
            pltpu.VMEM((slots * BS, GROUP * LANES), jnp.bfloat16),
            pltpu.SemaphoreType.DMA((count,)),
            pltpu.SemaphoreType.DMA((pieces, CHUNKS)),
            pltpu.SemaphoreType.DMA((10,)),
            pltpu.SemaphoreType.DMA((pieces,)),
            pltpu.SemaphoreType.DMA,
        ],
        compiler_params=pltpu.CompilerParams(
            collective_id=0, has_side_effects=True, vmem_limit_bytes=56 * 1024 * 1024
        ),
        cost_estimate=pl.CostEstimate(
            flops=2 * rows * slots * slots * BS**3,
            bytes_accessed=6 * rows * slots * area,
            transcendentals=0,
        ),
    )(
        place,
        right_blocks.reshape(rows * slots, BS, BS),
        left_blocks.reshape(rows * slots, BS, BS),
        codes,
        targets,
    )
    return out.reshape(cells_x, cells_y, slots, area)


def solution(mesh):
    placed = (
        P(("win", "col"), "row", None, None),
        P(("win", "col"), "row", None, None),
        P(("win", "col"), "row", None),
        P(("win", "col"), "row", None),
        P(("win", "col"), "row", None),
    )
    return jax.shard_map(
        body,
        mesh=mesh,
        in_specs=placed,
        out_specs=P(("win", "col"), "row", None, None),
        check_vma=False,
    )
```

```python
import functools

import jax
import jax.numpy as jnp
from jax import lax
from jax.experimental import pallas as pl
from jax.experimental.pallas import tpu as pltpu
from jax.sharding import PartitionSpec as P

BS = 96
LANES = 128
REACH = 2
GROUP = 2


HALF = BS // 2
PAIR_ROWS = 3 * HALF
WIDE = 64
CHUNKS = 2
MESH = pl.DeviceIdType.MESH


def pack(first, second):
    parts = [first[:HALF, :WIDE], first[HALF:, :WIDE]]
    others = [second[:HALF, :WIDE], second[HALF:, :WIDE]]
    narrow = [t[h : h + HALF, WIDE:] for t in (first, second) for h in (0, HALF)]
    return [jnp.concatenate(p, axis=1) for p in (parts, others, narrow)]


def unpack(rows_0, rows_1, narrow):
    step = BS - WIDE
    return [
        jnp.concatenate(
            [rows[:, h * WIDE : (h + 1) * WIDE], narrow[:, n * step : (n + 1) * step]], axis=1
        )
        for n, (rows, h) in enumerate(((rows_0, 0), (rows_0, 1), (rows_1, 0), (rows_1, 1)))
    ]


def near_kernel(
    cells_y, slots, peers_col, peers_row,
    place, turn_of, tiles, left, codes, targets,
    out,
    packed, near, near_codes, table_rows, table, stacked, partial, wide_a, wide_b, *sems,
):
    send_sems, recv_sems, code_send, code_recv, table_sem = sems
    col = lax.axis_index("col")
    row = lax.axis_index("row")
    up = {"col": lax.rem(col + 1, peers_col)}
    down = {"col": lax.rem(col + peers_col - 1, peers_col)}
    right = {"row": lax.rem(row + 1, peers_row)}
    back = {"row": lax.rem(row + peers_row - 1, peers_row)}
    pairs = slots // 2
    piece_pairs = packed.shape[1]
    span = piece_pairs // CHUNKS
    cells = REACH * REACH
    rows = out.shape[0]

    barrier = pltpu.get_barrier_semaphore()
    for peer in (up, down, right, back):
        pl.semaphore_signal(barrier, inc=1, device_id=peer, device_id_type=MESH)

    def pack_half(half):
        for x in range(REACH):
            for y in range(REACH):
                source = (x * cells_y + half * REACH + y) * slots
                target = (x * REACH + y) * pairs

                def one(p, carry):
                    first, second = tiles[source + 2 * p], tiles[source + 2 * p + 1]
                    for n, block in enumerate(pack(first, second)):
                        packed[5 + half, target + p, n * HALF : (n + 1) * HALF, :] = block
                    at = ((5 + half) * piece_pairs + target + p) * 2
                    near[at] = first
                    near[at + 1] = second
                    return carry

                lax.fori_loop(0, pairs, one, 0)

    def unpack_chunk(at_piece, chunk):
        def one(p, carry):
            blocks = [
                packed[at_piece, chunk * span + p, k * HALF : (k + 1) * HALF, :] for k in range(3)
            ]
            at = (at_piece * piece_pairs + chunk * span + p) * 2
            for k, half in enumerate(unpack(*blocks)):
                near[at + k // 2, (k % 2) * HALF : (k % 2 + 1) * HALF, :] = half
            return carry

        lax.fori_loop(0, span, one, 0)

    def move(to, chunk, source, device, count):
        part = pl.ds(chunk * span, span)
        return pltpu.make_async_remote_copy(
            src_ref=packed.at[source, part],
            dst_ref=packed.at[to, part],
            send_sem=send_sems.at[count],
            recv_sem=recv_sems.at[to, chunk],
            device_id=device,
            device_id_type=MESH,
        )

    def move_code(to, source, device, count):
        return pltpu.make_async_remote_copy(
            src_ref=source,
            dst_ref=near_codes.at[pl.ds(to * cells, cells)],
            send_sem=code_send.at[count],
            recv_sem=code_recv.at[to],
            device_id=device,
            device_id_type=MESH,
        )

    first_hop = [(0, 1, 0, up), (2, 1, 0, down), (0, 2, 1, up), (2, 2, 1, down)]
    side_hop = [(1, 3, 0, back), (1, 0, 1, right)]
    code_moves = []
    for px, py, half, device in first_hop + side_hop:
        code_moves.append(move_code(px * 4 + py, codes.at[half], device, len(code_moves)))
    moves = []
    order = []
    for n in range(0, len(first_hop), 2):
        for chunk in range(CHUNKS):
            for px, py, half, device in first_hop[n : n + 2]:
                m = move(px * 4 + py, chunk, 5 + half, device, len(moves))
                moves.append(m)
                order.append((m, px, py, chunk))
    sides = []
    for px, py, half, device in side_hop:
        for chunk in range(CHUNKS):
            m = move(px * 4 + py, chunk, 5 + half, device, len(moves))
            moves.append(m)
            sides.append((m, px * 4 + py, chunk))

    pack_half(0)
    pl.semaphore_wait(barrier, 4)
    ahead = 2 * CHUNKS
    for m in code_moves:
        m.start()
    for m, *_ in order[:ahead]:
        m.start()
    for m, *_ in sides[:CHUNKS]:
        m.start()
    pack_half(1)
    for m, *_ in sides[CHUNKS:]:
        m.start()

    late_counts = (9, 6)

    def row_of(j, kind):
        return (j // REACH) * cells_y + kind * REACH + j % REACH

    def spans(kind):
        late = late_counts[kind]
        start = -(-late * BS // LANES) * LANES
        return ((0, late, 0), (late, slots, start))

    def stack_rows(kind):
        def one(j, carry):
            i = row_of(j, kind)
            for first, last, start in spans(kind):
                for g in range(first, last, 4):
                    parts = [
                        left[i * slots + turn_of[i * slots + u]] for u in range(g, min(g + 4, last))
                    ]
                    at = start + (g - first) * BS
                    block = parts[0] if len(parts) == 1 else jnp.concatenate(parts, axis=1)
                    stacked[i, :, at : at + len(parts) * BS] = block
            return carry

        lax.fori_loop(0, rows // 2, one, 0)

    near_codes[5 * cells : 7 * cells] = codes[...].reshape(2 * cells, *codes.shape[2:])
    code_forwards = []
    for n, (px, py, half, device) in enumerate(first_hop):
        code_moves[n].wait_recv()
        to, device = ((px * 4 + 3), back) if py == 1 else (px * 4, right)
        source = near_codes.at[pl.ds((px * 4 + py) * cells, cells)]
        m = move_code(to, source, device, len(code_moves) + n)
        m.start()
        code_forwards.append(m)
    stack_rows(0)
    stack_rows(1)
    for m in code_moves[4:] + code_forwards:
        m.wait_recv()

    slot_rows = lax.broadcasted_iota(jnp.int32, (slots, LANES), 0)

    def table_row(n, carry):
        at = place[n]
        held = near_codes[jnp.maximum(at, 0)]
        match = (lax.shift_right_logical(held, 1) == targets[n // slots]) & ((held & 1) == 1)
        found = jnp.max(jnp.where(match, slot_rows + 1, 0), axis=0, keepdims=True)
        good = (found > 0) & (at >= 0)
        table_rows[pl.ds(n, 1)] = jnp.where(good, at * slots + found - 1, -1)
        return carry

    lax.fori_loop(0, rows * slots, table_row, 0)
    table_copy = pltpu.make_async_copy(table_rows, table, table_sem)
    table_copy.start()

    buffers = (wide_a, wide_b)

    def product_rows(kind, early):
        first, last, start = spans(kind)[early]
        depth = (last - first) * BS

        def one(j, carry):
            i = row_of(j, kind)
            lhs = stacked[i, :, start : start + depth]
            for turn in range(slots // GROUP):
                wide = buffers[turn % 2]
                for g in range(first, last):
                    for u in range(GROUP):
                        at = table[i * slots + g, turn * GROUP + u]
                        tile = near[jnp.maximum(at, 0)]
                        tile = jnp.where(at >= 0, tile, jnp.zeros_like(tile))
                        down_to = (g - first) * BS
                        wide[down_to : down_to + BS, u * LANES : u * LANES + BS] = tile
                total = jnp.dot(lhs, wide[:depth], preferred_element_type=jnp.float32)
                if early:
                    partial[i, turn] = total
                else:
                    total = (0.5 * (total + partial[i, turn])).astype(out.dtype)
                    for u in range(GROUP):
                        out[i, turn * GROUP + u] = total[:, u * LANES : u * LANES + BS]
            return carry

        lax.fori_loop(0, rows // 2, one, 0)

    wide_a[...] = jnp.zeros_like(wide_a)
    wide_b[...] = jnp.zeros_like(wide_b)
    forwards = []
    for n, (m, px, py, chunk) in enumerate(order):
        m.wait_recv()
        to, device = ((px * 4 + 3), back) if py == 1 else (px * 4, right)
        f = move(to, chunk, px * 4 + py, device, len(moves) + n)
        f.start()
        forwards.append((f, to, chunk))
        if n + ahead < len(order):
            order[n + ahead][0].start()
        unpack_chunk(px * 4 + py, chunk)
        if n < len(sides):
            sides[n][0].wait_recv()
            unpack_chunk(*sides[n][1:])
        if n >= 2:
            forwards[n - 2][0].wait_recv()
            unpack_chunk(*forwards[n - 2][1:])
        if n == 2 * CHUNKS + 1:
            table_copy.wait()
            product_rows(0, 1)
        if n == 2 * CHUNKS + 2:
            product_rows(1, 1)
    for f, to, chunk in forwards[-2:]:
        f.wait_recv()
        unpack_chunk(to, chunk)
    product_rows(0, 0)
    product_rows(1, 0)
    for m in moves + [f for f, *_ in forwards] + code_moves + code_forwards:
        m.wait_send()


def body(left_blocks, right_blocks, pattern, left_live, right_live):
    cells_x, cells_y, slots, area = left_blocks.shape
    rows = cells_x * cells_y
    assert cells_x == REACH and cells_y == 2 * REACH
    peers_col = lax.axis_size("col")
    peers_row = lax.axis_size("row")
    grid_x = cells_x * peers_col
    grid_y = cells_y * peers_row
    cells = REACH * REACH
    pieces = 12
    piece_pairs = cells * slots // 2
    vmem = pl.BlockSpec(memory_space=pltpu.VMEM)

    codes = pattern * 2 + (right_live != 0).astype(jnp.int32)
    codes = jnp.stack([codes[:, :REACH], codes[:, REACH:]]).reshape(2, cells, slots, 1)
    codes = jnp.broadcast_to(codes, (2, cells, slots, LANES))

    local_x = jnp.arange(cells_x, dtype=jnp.int32)[:, None, None]
    local_y = jnp.arange(cells_y, dtype=jnp.int32)[None, :, None]
    own_x = lax.axis_index("col") * cells_x + local_x
    own_y = lax.axis_index("row") * cells_y + local_y
    near_x = local_x + (pattern // grid_y - own_x + REACH) % grid_x
    near_y = local_y + (pattern % grid_y - own_y + REACH) % grid_y
    piece = (near_x // REACH) * 4 + near_y // REACH
    place = piece * cells + (near_x % REACH) * REACH + near_y % REACH
    last = (piece // 4 != 1) & (piece % 2 == 0)
    key = jnp.where(last, 0, slots).reshape(rows, slots) + jnp.arange(slots, dtype=jnp.int32)
    rank = jnp.sum(key[:, None, :] < key[:, :, None], axis=2, dtype=jnp.int32)
    hit = rank[:, None, :] == jnp.arange(slots, dtype=jnp.int32)[None, :, None]
    turn_of = jnp.where(hit, jnp.arange(slots, dtype=jnp.int32), 0).sum(axis=2).reshape(-1)
    place = jnp.where(left_live != 0, place, -1).reshape(rows, 1, slots)
    place = jnp.where(hit, place, 0).sum(axis=2).reshape(-1)
    targets = jnp.pad(
        pattern.reshape(rows, 1, slots), ((0, 0), (0, 0), (0, LANES - slots)), constant_values=-1
    )

    count = 10 * CHUNKS
    out = pl.pallas_call(
        functools.partial(near_kernel, cells_y, slots, peers_col, peers_row),
        out_shape=jax.ShapeDtypeStruct((rows, slots, BS, BS), jnp.bfloat16),
        in_specs=[pl.BlockSpec(memory_space=pltpu.SMEM)] * 2 + [vmem] * 4,
        out_specs=vmem,
        scratch_shapes=[
            pltpu.VMEM((pieces, piece_pairs, PAIR_ROWS, LANES), jnp.bfloat16),
            pltpu.VMEM((pieces * cells * slots, BS, BS), jnp.bfloat16),
            pltpu.VMEM((pieces * cells, slots, LANES), jnp.int32),
            pltpu.VMEM((rows * slots, LANES), jnp.int32),
            pltpu.SMEM((rows * slots, LANES), jnp.int32),
            pltpu.VMEM((rows, BS, slots * BS + LANES), jnp.bfloat16),
            pltpu.VMEM((rows, slots // GROUP, BS, GROUP * LANES), jnp.float32),
            pltpu.VMEM((slots * BS, GROUP * LANES), jnp.bfloat16),
            pltpu.VMEM((slots * BS, GROUP * LANES), jnp.bfloat16),
            pltpu.SemaphoreType.DMA((count,)),
            pltpu.SemaphoreType.DMA((pieces, CHUNKS)),
            pltpu.SemaphoreType.DMA((10,)),
            pltpu.SemaphoreType.DMA((pieces,)),
            pltpu.SemaphoreType.DMA,
        ],
        compiler_params=pltpu.CompilerParams(
            collective_id=0, has_side_effects=True, vmem_limit_bytes=58 * 1024 * 1024
        ),
        cost_estimate=pl.CostEstimate(
            flops=2 * rows * slots * slots * BS**3,
            bytes_accessed=6 * rows * slots * area,
            transcendentals=0,
        ),
    )(
        place,
        turn_of,
        right_blocks.reshape(rows * slots, BS, BS),
        left_blocks.reshape(rows * slots, BS, BS),
        codes,
        targets,
    )
    return out.reshape(cells_x, cells_y, slots, area)


def solution(mesh):
    placed = (
        P(("win", "col"), "row", None, None),
        P(("win", "col"), "row", None, None),
        P(("win", "col"), "row", None),
        P(("win", "col"), "row", None),
        P(("win", "col"), "row", None),
    )
    return jax.shard_map(
        body,
        mesh=mesh,
        in_specs=placed,
        out_specs=P(("win", "col"), "row", None, None),
        check_vma=False,
    )
```

```python
import functools

import jax
import jax.numpy as jnp
from jax import lax
from jax.experimental import pallas as pl
from jax.experimental.pallas import tpu as pltpu
from jax.sharding import PartitionSpec as P

BS = 96
LANES = 128
REACH = 2
GROUP = 2


HALF = BS // 2
PAIR_ROWS = 3 * HALF
WIDE = 64
CHUNKS = 4
MESH = pl.DeviceIdType.MESH


def pack(first, second):
    parts = [first[:HALF, :WIDE], first[HALF:, :WIDE]]
    others = [second[:HALF, :WIDE], second[HALF:, :WIDE]]
    narrow = [t[h : h + HALF, WIDE:] for t in (first, second) for h in (0, HALF)]
    return [jnp.concatenate(p, axis=1) for p in (parts, others, narrow)]


def unpack(rows_0, rows_1, narrow):
    step = BS - WIDE
    return [
        jnp.concatenate(
            [rows[:, h * WIDE : (h + 1) * WIDE], narrow[:, n * step : (n + 1) * step]], axis=1
        )
        for n, (rows, h) in enumerate(((rows_0, 0), (rows_0, 1), (rows_1, 0), (rows_1, 1)))
    ]


def near_kernel(
    cells_y, slots, peers_col, peers_row,
    place, turn_of, tiles, left, codes, targets,
    out,
    packed, near, near_codes, table_rows, table, stacked, partial, wide_a, wide_b, *sems,
):
    send_sems, recv_sems, code_send, code_recv, table_sem = sems
    col = lax.axis_index("col")
    row = lax.axis_index("row")
    up = {"col": lax.rem(col + 1, peers_col)}
    down = {"col": lax.rem(col + peers_col - 1, peers_col)}
    right = {"row": lax.rem(row + 1, peers_row)}
    back = {"row": lax.rem(row + peers_row - 1, peers_row)}
    pairs = slots // 2
    piece_pairs = packed.shape[1]
    span = piece_pairs // CHUNKS
    cells = REACH * REACH
    rows = out.shape[0]

    barrier = pltpu.get_barrier_semaphore()
    for peer in (up, down, right, back):
        pl.semaphore_signal(barrier, inc=1, device_id=peer, device_id_type=MESH)

    def pack_half(half):
        for x in range(REACH):
            for y in range(REACH):
                source = (x * cells_y + half * REACH + y) * slots
                target = (x * REACH + y) * pairs

                def one(p, carry):
                    first, second = tiles[source + 2 * p], tiles[source + 2 * p + 1]
                    for n, block in enumerate(pack(first, second)):
                        packed[5 + half, target + p, n * HALF : (n + 1) * HALF, :] = block
                    at = ((5 + half) * piece_pairs + target + p) * 2
                    near[at] = first
                    near[at + 1] = second
                    return carry

                lax.fori_loop(0, pairs, one, 0)

    def unpack_chunk(at_piece, chunk):
        def one(p, carry):
            blocks = [
                packed[at_piece, chunk * span + p, k * HALF : (k + 1) * HALF, :] for k in range(3)
            ]
            at = (at_piece * piece_pairs + chunk * span + p) * 2
            for k, half in enumerate(unpack(*blocks)):
                near[at + k // 2, (k % 2) * HALF : (k % 2 + 1) * HALF, :] = half
            return carry

        lax.fori_loop(0, span, one, 0)

    def move(to, chunk, source, device, count):
        part = pl.ds(chunk * span, span)
        return pltpu.make_async_remote_copy(
            src_ref=packed.at[source, part],
            dst_ref=packed.at[to, part],
            send_sem=send_sems.at[count],
            recv_sem=recv_sems.at[to, chunk],
            device_id=device,
            device_id_type=MESH,
        )

    def move_code(to, source, device, count):
        return pltpu.make_async_remote_copy(
            src_ref=source,
            dst_ref=near_codes.at[pl.ds(to * cells, cells)],
            send_sem=code_send.at[count],
            recv_sem=code_recv.at[to],
            device_id=device,
            device_id_type=MESH,
        )

    first_hop = [(0, 1, 0, up), (2, 1, 0, down), (0, 2, 1, up), (2, 2, 1, down)]
    side_hop = [(1, 3, 0, back), (1, 0, 1, right)]
    code_moves = []
    for px, py, half, device in first_hop + side_hop:
        code_moves.append(move_code(px * 4 + py, codes.at[half], device, len(code_moves)))
    moves = []
    order = []
    for n in range(0, len(first_hop), 2):
        for chunk in range(CHUNKS):
            for px, py, half, device in first_hop[n : n + 2]:
                m = move(px * 4 + py, chunk, 5 + half, device, len(moves))
                moves.append(m)
                order.append((m, px, py, chunk))
    sides = []
    for px, py, half, device in side_hop:
        for chunk in range(CHUNKS):
            m = move(px * 4 + py, chunk, 5 + half, device, len(moves))
            moves.append(m)
            sides.append((m, px * 4 + py, chunk))

    pack_half(0)
    pl.semaphore_wait(barrier, 4)
    ahead = 2 * CHUNKS
    for m in code_moves:
        m.start()
    for m, *_ in order[:ahead]:
        m.start()
    for m, *_ in sides[:CHUNKS]:
        m.start()
    pack_half(1)
    for m, *_ in sides[CHUNKS:]:
        m.start()

    late_counts = (9, 6)

    def row_of(j, kind):
        return (j // REACH) * cells_y + kind * REACH + j % REACH

    def spans(kind):
        late = late_counts[kind]
        start = -(-late * BS // LANES) * LANES
        return ((0, late, 0), (late, slots, start))

    def stack_rows(kind):
        def one(j, carry):
            i = row_of(j, kind)
            for first, last, start in spans(kind):
                for g in range(first, last, 4):
                    parts = [
                        left[i * slots + turn_of[i * slots + u]] for u in range(g, min(g + 4, last))
                    ]
                    at = start + (g - first) * BS
                    block = parts[0] if len(parts) == 1 else jnp.concatenate(parts, axis=1)
                    stacked[i, :, at : at + len(parts) * BS] = block
            return carry

        lax.fori_loop(0, rows // 2, one, 0)

    near_codes[5 * cells : 7 * cells] = codes[...].reshape(2 * cells, *codes.shape[2:])
    code_forwards = []
    for n, (px, py, half, device) in enumerate(first_hop):
        code_moves[n].wait_recv()
        to, device = ((px * 4 + 3), back) if py == 1 else (px * 4, right)
        source = near_codes.at[pl.ds((px * 4 + py) * cells, cells)]
        m = move_code(to, source, device, len(code_moves) + n)
        m.start()
        code_forwards.append(m)
    stack_rows(0)
    stack_rows(1)
    for m in code_moves[4:] + code_forwards:
        m.wait_recv()

    slot_rows = lax.broadcasted_iota(jnp.int32, (slots, LANES), 0)

    def table_row(n, carry):
        at = place[n]
        held = near_codes[jnp.maximum(at, 0)]
        match = (lax.shift_right_logical(held, 1) == targets[n // slots]) & ((held & 1) == 1)
        found = jnp.max(jnp.where(match, slot_rows + 1, 0), axis=0, keepdims=True)
        good = (found > 0) & (at >= 0)
        table_rows[pl.ds(n, 1)] = jnp.where(good, at * slots + found - 1, -1)
        return carry

    lax.fori_loop(0, rows * slots, table_row, 0)
    table_copy = pltpu.make_async_copy(table_rows, table, table_sem)
    table_copy.start()

    buffers = (wide_a, wide_b)

    def product_rows(kind, early):
        first, last, start = spans(kind)[early]
        depth = (last - first) * BS

        def one(j, carry):
            i = row_of(j, kind)
            lhs = stacked[i, :, start : start + depth]
            for turn in range(slots // GROUP):
                wide = buffers[turn % 2]
                for g in range(first, last):
                    for u in range(GROUP):
                        at = table[i * slots + g, turn * GROUP + u]
                        tile = near[jnp.maximum(at, 0)]
                        tile = jnp.where(at >= 0, tile, jnp.zeros_like(tile))
                        down_to = (g - first) * BS
                        wide[down_to : down_to + BS, u * LANES : u * LANES + BS] = tile
                total = jnp.dot(lhs, wide[:depth], preferred_element_type=jnp.float32)
                if early:
                    partial[i, turn] = total
                else:
                    total = (0.5 * (total + partial[i, turn])).astype(out.dtype)
                    for u in range(GROUP):
                        out[i, turn * GROUP + u] = total[:, u * LANES : u * LANES + BS]
            return carry

        lax.fori_loop(0, rows // 2, one, 0)

    wide_a[...] = jnp.zeros_like(wide_a)
    wide_b[...] = jnp.zeros_like(wide_b)
    forwards = []
    for n, (m, px, py, chunk) in enumerate(order):
        m.wait_recv()
        to, device = ((px * 4 + 3), back) if py == 1 else (px * 4, right)
        f = move(to, chunk, px * 4 + py, device, len(moves) + n)
        f.start()
        forwards.append((f, to, chunk))
        if n + ahead < len(order):
            order[n + ahead][0].start()
        unpack_chunk(px * 4 + py, chunk)
        if n < len(sides):
            sides[n][0].wait_recv()
            unpack_chunk(*sides[n][1:])
        if n >= 2:
            forwards[n - 2][0].wait_recv()
            unpack_chunk(*forwards[n - 2][1:])
        if n == 2 * CHUNKS + 1:
            table_copy.wait()
            product_rows(0, 1)
        if n == 2 * CHUNKS + 2:
            product_rows(1, 1)
    for f, to, chunk in forwards[-2:]:
        f.wait_recv()
        unpack_chunk(to, chunk)
    product_rows(0, 0)
    product_rows(1, 0)
    for m in moves + [f for f, *_ in forwards] + code_moves + code_forwards:
        m.wait_send()


def body(left_blocks, right_blocks, pattern, left_live, right_live):
    cells_x, cells_y, slots, area = left_blocks.shape
    rows = cells_x * cells_y
    assert cells_x == REACH and cells_y == 2 * REACH
    peers_col = lax.axis_size("col")
    peers_row = lax.axis_size("row")
    grid_x = cells_x * peers_col
    grid_y = cells_y * peers_row
    cells = REACH * REACH
    pieces = 12
    piece_pairs = cells * slots // 2
    vmem = pl.BlockSpec(memory_space=pltpu.VMEM)

    codes = pattern * 2 + (right_live != 0).astype(jnp.int32)
    codes = jnp.stack([codes[:, :REACH], codes[:, REACH:]]).reshape(2, cells, slots, 1)
    codes = jnp.broadcast_to(codes, (2, cells, slots, LANES))

    local_x = jnp.arange(cells_x, dtype=jnp.int32)[:, None, None]
    local_y = jnp.arange(cells_y, dtype=jnp.int32)[None, :, None]
    own_x = lax.axis_index("col") * cells_x + local_x
    own_y = lax.axis_index("row") * cells_y + local_y
    near_x = local_x + (pattern // grid_y - own_x + REACH) % grid_x
    near_y = local_y + (pattern % grid_y - own_y + REACH) % grid_y
    piece = (near_x // REACH) * 4 + near_y // REACH
    place = piece * cells + (near_x % REACH) * REACH + near_y % REACH
    last = (piece // 4 != 1) & (piece % 2 == 0)
    key = jnp.where(last, 0, slots).reshape(rows, slots) + jnp.arange(slots, dtype=jnp.int32)
    rank = jnp.sum(key[:, None, :] < key[:, :, None], axis=2, dtype=jnp.int32)
    hit = rank[:, None, :] == jnp.arange(slots, dtype=jnp.int32)[None, :, None]
    turn_of = jnp.where(hit, jnp.arange(slots, dtype=jnp.int32), 0).sum(axis=2).reshape(-1)
    place = jnp.where(left_live != 0, place, -1).reshape(rows, 1, slots)
    place = jnp.where(hit, place, 0).sum(axis=2).reshape(-1)
    targets = jnp.pad(
        pattern.reshape(rows, 1, slots), ((0, 0), (0, 0), (0, LANES - slots)), constant_values=-1
    )

    count = 10 * CHUNKS
    out = pl.pallas_call(
        functools.partial(near_kernel, cells_y, slots, peers_col, peers_row),
        out_shape=jax.ShapeDtypeStruct((rows, slots, BS, BS), jnp.bfloat16),
        in_specs=[pl.BlockSpec(memory_space=pltpu.SMEM)] * 2 + [vmem] * 4,
        out_specs=vmem,
        scratch_shapes=[
            pltpu.VMEM((pieces, piece_pairs, PAIR_ROWS, LANES), jnp.bfloat16),
            pltpu.VMEM((pieces * cells * slots, BS, BS), jnp.bfloat16),
            pltpu.VMEM((pieces * cells, slots, LANES), jnp.int32),
            pltpu.VMEM((rows * slots, LANES), jnp.int32),
            pltpu.SMEM((rows * slots, LANES), jnp.int32),
            pltpu.VMEM((rows, BS, slots * BS + LANES), jnp.bfloat16),
            pltpu.VMEM((rows, slots // GROUP, BS, GROUP * LANES), jnp.float32),
            pltpu.VMEM((slots * BS, GROUP * LANES), jnp.bfloat16),
            pltpu.VMEM((slots * BS, GROUP * LANES), jnp.bfloat16),
            pltpu.SemaphoreType.DMA((count,)),
            pltpu.SemaphoreType.DMA((pieces, CHUNKS)),
            pltpu.SemaphoreType.DMA((10,)),
            pltpu.SemaphoreType.DMA((pieces,)),
            pltpu.SemaphoreType.DMA,
        ],
        compiler_params=pltpu.CompilerParams(
            collective_id=0, has_side_effects=True, vmem_limit_bytes=58 * 1024 * 1024
        ),
        cost_estimate=pl.CostEstimate(
            flops=2 * rows * slots * slots * BS**3,
            bytes_accessed=6 * rows * slots * area,
            transcendentals=0,
        ),
    )(
        place,
        turn_of,
        right_blocks.reshape(rows * slots, BS, BS),
        left_blocks.reshape(rows * slots, BS, BS),
        codes,
        targets,
    )
    return out.reshape(cells_x, cells_y, slots, area)


def solution(mesh):
    placed = (
        P(("win", "col"), "row", None, None),
        P(("win", "col"), "row", None, None),
        P(("win", "col"), "row", None),
        P(("win", "col"), "row", None),
        P(("win", "col"), "row", None),
    )
    return jax.shard_map(
        body,
        mesh=mesh,
        in_specs=placed,
        out_specs=P(("win", "col"), "row", None, None),
        check_vma=False,
    )
```
